256 devices in a mesh: dp: 32 (over z, y), head: 8 (over x, core).
Axes of the slice: x: 4, y: 4, z: 8, core: 2. Of those that a mesh axis runs over, the one named last changes fastest.
Arguments:
- memory: bfloat16 [61440, 2048], P('dp'), may hold values from -6 to 6
- block_route: int32 [2, 480], P(None, 'dp'), may hold values from 0 to 31, as said below
- enc_len: int32 [192], P('dp'), may hold values from 1 to 512, as said below
- w_key: bfloat16 [2048, 2048], P(None, 'head'), may hold values from -0.125 to 0.125
- w_value: bfloat16 [2048, 2048], P(None, 'head'), may hold values from -0.125 to 0.125
- dec_query: bfloat16 [192, 2048], P('dp', 'head'), may hold values from -60 to 60
- dec_hidden: bfloat16 [192, 2048], P('dp', 'head'), may hold values from -1.5 to 1.5
- w_out: bfloat16 [2048, 2048], P('head'), may hold values from -0.125 to 0.125
Outputs:
- new_hidden: bfloat16 [192, 2048], P('dp', 'head')
- key_grid: bfloat16 [192, 512, 2048], P('dp', None, 'head')
- value_grid: bfloat16 [192, 512, 2048], P('dp', None, 'head')
The draws below stay inside these ranges and needn't reach their ends.
Inputs may be any that keep to these rules, and one draw needn't show every extreme that they name: `enc_len`: request i belongs to home group i // 6. It has n_i = ceil(enc_len_i / 128) blocks, 1 to 4; the blocks of each home group sum to 30 minus those of its paired group, and every request has a request with 4 full blocks in its pair of groups. `block_route`: each home group's used cells (r * 4 + b with b < n of request r) appear exactly once over all slots, other cells never. Each slot holds 15 blocks and sends at most 1 of them to one home group; some slot sends exactly 1 to some group.
All inputs are finite; a program needn't handle non-finite values.
Results may differ from the reference program's by a relative error of at most 0.012.
The reference program's roundings to bfloat16 on the way (of `attention` and `context`) count: a program that leaves them out, or rounds other values in their place, can miss the bound.
Values may be sent and summed in bfloat16 or wider, within the bound.
A program may use at most 128 MiB of HBM per device.

```python
import jax
import jax.numpy as jnp
from jax import lax

D = 2048
HEADS = 32
HEAD_DIM = 64
BLOCK = 128
MAXB = 4
REQ_DEV = 6
HQ = 2048
SLOT_BLOCKS = 15
REQUESTS = 192
ALL_BLOCKS = 480
N_DP = 32


def block_counts(key):
    key_pair, key_base, key_long = jax.random.split(key, 3)
    pairing = jax.random.permutation(key_pair, N_DP)
    counts_drawn = jax.random.randint(key_base, (N_DP // 2, REQ_DEV), 1, MAXB + 1)
    long_slot = jax.random.randint(key_long, (N_DP // 2,), 0, REQ_DEV)
    long_mask = jnp.arange(REQ_DEV)[None, :] == long_slot[:, None]
    first_home = jnp.where(long_mask, MAXB, counts_drawn)
    second_home = MAXB + 1 - first_home
    counts = jnp.zeros((N_DP, REQ_DEV), jnp.int32)
    counts = counts.at[pairing[0::2]].set(first_home).at[pairing[1::2]].set(second_home)
    is_full = jnp.zeros((N_DP, REQ_DEV), jnp.bool_).at[pairing[0::2]].set(long_mask)
    return (counts, is_full)


def draw_enc_len(key, part):
    counts, is_full = block_counts(key)
    key = jax.random.fold_in(key, 11)
    last_rows = jax.random.randint(key, (N_DP, REQ_DEV), 1, BLOCK + 1)
    last_rows = jnp.where(is_full, BLOCK, last_rows)
    return (BLOCK * (counts - 1) + last_rows).reshape(-1).astype(jnp.int32)


def draw_block_route(key, part):
    counts, is_full = block_counts(key)
    key = jax.random.fold_in(key, 12)
    key_slot, key_shift = jax.random.split(key)
    block_total = N_DP * SLOT_BLOCKS
    block_index = jnp.arange(MAXB)[None, None, :]
    used = (block_index < counts[:, :, None]).reshape(-1)
    running = jnp.cumsum(used.astype(jnp.int32)) - 1
    slot_perm = jax.random.permutation(key_slot, N_DP)
    slot_shift = jax.random.randint(key_shift, (N_DP,), 0, SLOT_BLOCKS)
    slot_of = slot_perm[running % N_DP]
    place_in = (running // N_DP + slot_shift[slot_of]) % SLOT_BLOCKS
    targets = jnp.where(used, slot_of * SLOT_BLOCKS + place_in, block_total)
    home_ids = jnp.repeat(jnp.arange(N_DP, dtype=jnp.int32), REQ_DEV * MAXB)
    grid_cells = jnp.tile(jnp.arange(REQ_DEV * MAXB, dtype=jnp.int32), N_DP)
    routed = jnp.zeros((2, block_total + 1), jnp.int32)
    routed = routed.at[0, targets].set(home_ids).at[1, targets].set(grid_cells)
    return routed[:, :block_total]


def draw_dec_query(key, part):
    key = jax.random.fold_in(key, 13)
    key_vals = jax.random.fold_in(key, 0)
    drawn = jax.random.normal(key_vals, (REQ_DEV * N_DP, HEADS * HEAD_DIM), jnp.float32)
    drawn = drawn * 0.25
    return drawn.astype(jnp.bfloat16)


def block_levels(own_key, extent, pieces, low, high):
    factor_of = 1.0
    for axis_at, shards_of in pieces:
        steps = jax.random.uniform(jax.random.fold_in(jax.random.fold_in(own_key, 6), axis_at), (shards_of,), jnp.float32, low / len(pieces), high / len(pieces))
        factor_of = factor_of * jnp.repeat(jnp.exp(steps), extent[axis_at] // shards_of).reshape((-1,) + (1,) * (len(extent) - 1 - axis_at))
    return factor_of


def gaussian(key, dims, width, limit, pieces=(), held_as=jnp.bfloat16):
    loudness = block_levels(key, dims, pieces, -0.22, 0.18) if pieces else 1.0
    array = jax.random.normal(key, dims, jnp.float32) * width * loudness
    return jnp.minimum(jnp.maximum(array, -limit), limit).astype(held_as)


def setup_inputs(seed: int = 0) -> dict:
    arg_keys = jax.random.split(jax.random.key(seed), 9)
    memory = gaussian(arg_keys[0], (ALL_BLOCKS * BLOCK, D), 1.0, 6.0, ((0, 32),))
    block_route = draw_block_route(jax.random.fold_in(arg_keys[8], 71), 0)
    enc_len = draw_enc_len(jax.random.fold_in(arg_keys[8], 71), 0)
    w_key = gaussian(arg_keys[3], (D, HQ), D ** -0.5, 0.125, ((1, 8),))
    w_value = gaussian(arg_keys[4], (D, HQ), D ** -0.5, 0.125, ((1, 8),))
    dec_query = draw_dec_query(jax.random.fold_in(arg_keys[8], 71), 0)
    dec_hidden = gaussian(arg_keys[6], (REQUESTS, D), 0.25, 1.5, ((0, 32), (1, 8)))
    w_out = gaussian(arg_keys[7], (HQ, D), HQ ** -0.5, 0.125, ((0, 8),))
    return {"memory": memory, "block_route": block_route, "enc_len": enc_len, "w_key": w_key, "w_value": w_value, "dec_query": dec_query, "dec_hidden": dec_hidden, "w_out": w_out}


def reference(memory, block_route, enc_len, w_key, w_value, dec_query, dec_hidden, w_out):
    grid_size = REQ_DEV * MAXB
    span = MAXB * BLOCK
    key_rows = jnp.dot(memory, w_key, preferred_element_type=jnp.float32).astype(jnp.bfloat16)
    value_rows = jnp.dot(memory, w_value, preferred_element_type=jnp.float32).astype(jnp.bfloat16)
    targets = (block_route[0] * grid_size + block_route[1]).astype(jnp.int32)

    def to_grid(row_data):
        blocks = row_data.reshape(N_DP * SLOT_BLOCKS, BLOCK, HQ)
        placed = jnp.zeros((N_DP * grid_size, BLOCK, HQ), jnp.bfloat16).at[targets].set(blocks)
        return placed.reshape(N_DP, REQ_DEV, span, HEADS, HEAD_DIM)

    key_grid = to_grid(key_rows)
    value_grid = to_grid(value_rows)
    queries = dec_query.reshape(N_DP, REQ_DEV, HEADS, HEAD_DIM)
    lengths = enc_len.reshape(N_DP, REQ_DEV)

    def one_home(items):
        key_part, value_part, query_part, length_part = items
        scores = jnp.einsum("rhd,rshd->rhs", query_part.astype(jnp.float32), key_part.astype(jnp.float32))
        is_valid = jnp.arange(span)[None, None, :] < length_part[:, None, None]
        scores = jnp.where(is_valid, scores, -1e30)
        peak = jnp.max(scores, axis=2, keepdims=True)
        expo = jnp.exp(scores - peak)
        attention = (expo / jnp.sum(expo, axis=2, keepdims=True)).astype(jnp.bfloat16)
        context = jnp.einsum("rhs,rshd->rhd", attention.astype(jnp.float32), value_part.astype(jnp.float32))
        return context.astype(jnp.bfloat16).reshape(REQ_DEV, HQ)

    contexts = lax.map(one_home, (key_grid, value_grid, queries, lengths))
    mixed = jnp.dot(contexts.reshape(N_DP * REQ_DEV, HQ), w_out, preferred_element_type=jnp.float32)
    new_hidden = (dec_hidden.astype(jnp.float32) + mixed).astype(jnp.bfloat16)
    key_out = key_grid.reshape(N_DP * REQ_DEV, span, HQ)
    value_out = value_grid.reshape(N_DP * REQ_DEV, span, HQ)
    return (new_hidden, key_out, value_out)
```

```python
import functools

import jax
import jax.numpy as jnp
from jax import lax
from jax.experimental import pallas as pl
from jax.experimental.pallas import tpu as pltpu
from jax.sharding import PartitionSpec as P

HEAD_DIM = 64
BLOCK = 128
MAXB = 4
ZN, YN, XN, CN = 8, 4, 4, 2
NDP, NHEAD = ZN * YN, XN * CN
RM = 112
RK = BLOCK - RM
GROUP = 2
NGROUP = NDP // GROUP
LAG = 2
MESH = pl.DeviceIdType.MESH
BF16 = jnp.bfloat16


def slot_offset(k):
    i, j = k // YN, k % YN
    dz = (i % 2) * ((i + 1) // 2) + (1 - i % 2) * ((ZN - i // 2) % ZN)
    dy = (j % 2) * ((j + 1) // 2) + (1 - j % 2) * ((YN - j // 2) % YN)
    return dz, dy


def move_kernel(
    table, mem, wk, wv, kv_mem, kv_dir, tags,
    own, rest, rest_kv, wts, packed, kv_out, tag_out, pool,
    in_sem, a_send, a_recv, d_send, d_recv, t_send, t_recv,
    xp_send, xp_recv, xm_send, xm_recv, f_send, f_recv, c_send, c_recv,
):
    dp, head = lax.axis_index("dp"), lax.axis_index("head")
    z, y = dp // YN, dp % YN
    x, core = head // CN, head % CN
    right = ((x + 1) % XN) * CN + core
    left = ((x + XN - 1) % XN) * CN + core
    across = ((x + 2) % XN) * CN + core
    twin = x * CN + 1 - core

    def peer(k):
        dz, dy = slot_offset(k)
        return ((z + dz) % ZN) * YN + (y + dy) % YN

    loads = [
        pltpu.make_async_copy(mem.at[:, 0:RM, pl.ds(pl.multiple_of(head * 256, 256), 256)], own, in_sem.at[0]),
        pltpu.make_async_copy(mem.at[:, RM:BLOCK, :], rest, in_sem.at[1]),
        pltpu.make_async_copy(wk, wts.at[:, 0:256], in_sem.at[2]),
        pltpu.make_async_copy(wv, wts.at[:, 256:512], in_sem.at[3]),
    ]
    for load in loads:
        load.start()

    barrier = pltpu.get_barrier_semaphore()

    def greet(k, _):
        pl.semaphore_signal(barrier, inc=1, device_id=(peer(k), head), device_id_type=MESH)
        return 0

    lax.fori_loop(1, NDP, greet, 0)
    for other in (right, left, twin):
        pl.semaphore_signal(barrier, inc=1, device_id=(dp, other), device_id_type=MESH)

    loads[0].wait()

    def fill(k, _):
        home = peer(k)
        packed[k] = own[table[0, home]]
        tag_out[k] = jnp.full((8, 128), table[1, home], jnp.int32)
        return 0

    lax.fori_loop(0, NDP, fill, 0)
    pool[head, pl.ds(0, RM), :] = packed[0]
    tags[0] = tag_out[0]
    pl.semaphore_wait(barrier, NDP - 1 + 3)

    def rows_of(k, count):
        return pl.ds(pl.multiple_of(k * RM, 16), count * RM)

    def a_copy(k):
        return pltpu.make_async_remote_copy(
            src_ref=packed.at[k], dst_ref=pool.at[head, rows_of(k, 1), :],
            send_sem=a_send.at[k], recv_sem=a_recv.at[k],
            device_id=(peer(k), head), device_id_type=MESH)

    def t_copy(k):
        return pltpu.make_async_remote_copy(
            src_ref=tag_out.at[k], dst_ref=tags.at[k],
            send_sem=t_send.at[k], recv_sem=t_recv.at[k],
            device_id=(peer(k), head), device_id_type=MESH)

    def d_copy(k):
        return pltpu.make_async_remote_copy(
            src_ref=kv_out.at[k], dst_ref=kv_dir.at[k],
            send_sem=d_send.at[k], recv_sem=d_recv.at[k],
            device_id=(peer(k), head), device_id_type=MESH)

    def each(first, last, act):
        def step(k, _):
            act(k)
            return 0

        lax.fori_loop(first, last, step, 0)

    each(1, NDP, lambda k: a_copy(k).start())

    loads[1].wait()
    loads[2].wait()
    loads[3].wait()
    slots = rest.shape[0]
    rest_rows = rest[...].reshape(slots * RK, rest.shape[2])
    rest_kv[...] = (
        jnp.dot(rest_rows, wts[...], preferred_element_type=jnp.float32)
        .astype(BF16)
        .reshape(slots, RK, 512)
    )

    def send_direct(k):
        kv_out[k] = rest_kv[table[0, peer(k)]]
        d_copy(k).start()
        t_copy(k).start()

    each(1, NDP, send_direct)
    kv_dir[0] = rest_kv[table[0, dp]]

    def head_copy(piece, group, target, send, recv):
        where = pool.at[piece, rows_of(group * GROUP, GROUP), :]
        return pltpu.make_async_remote_copy(
            src_ref=where, dst_ref=where, send_sem=send, recv_sem=recv,
            device_id=(dp, target), device_id_type=MESH)

    def plus_copy(g):
        return head_copy(head, g, right, xp_send.at[g], xp_recv.at[g])

    def minus_copy(g):
        return head_copy(head, g, left, xm_send.at[g], xm_recv.at[g])

    def forward_right(g):
        return head_copy(left, g, right, f_send.at[g], f_recv.at[g])

    def forward_left(g):
        return head_copy(right, g, left, f_send.at[g], f_recv.at[g])

    def core_copy(piece, n, g):
        return head_copy(piece, g, twin, c_send.at[n, g], c_recv.at[n, g])

    def stage_own(g):
        def arrived(k):
            pl.when(k > 0)(lambda: a_copy(k).wait_recv())

        each(g * GROUP, (g + 1) * GROUP, arrived)
        plus_copy(g).start()
        minus_copy(g).start()
        core_copy(head, 0, g).start()

    def stage_forward(g):
        plus_copy(g).wait_recv()
        minus_copy(g).wait_recv()
        pl.when(g % 2 == 0)(lambda: forward_right(g).start())
        pl.when(g % 2 == 1)(lambda: forward_left(g).start())
        core_copy(left, 1, g).start()
        core_copy(right, 2, g).start()

    def stage_core(g):
        forward_right(g).wait_recv()
        core_copy(across, 3, g).start()

    def stage_project(g):
        for n in range(4):
            core_copy(head, n, g).wait_recv()
        rows = rows_of(g * GROUP, GROUP)
        block = jnp.concatenate([pool[p, rows, :] for p in range(NHEAD)], axis=1)
        kv_mem[rows, :] = jnp.dot(block, wts[...], preferred_element_type=jnp.float32).astype(BF16)

    def round_of(t):
        for late, stage in enumerate((stage_own, stage_forward, stage_core, stage_project)):
            g = t - late * LAG
            pl.when((g >= 0) & (g < NGROUP))(functools.partial(stage, g))

    each(0, NGROUP + 3 * LAG, round_of)

    def settle(k):
        a_copy(k).wait_send()
        d_copy(k).wait()
        t_copy(k).wait()

    each(1, NDP, settle)

    def settle_group(g):
        plus_copy(g).wait_send()
        minus_copy(g).wait_send()
        forward_right(g).wait_send()
        for n in range(4):
            core_copy(head, n, g).wait_send()

    each(0, NGROUP, settle_group)


def move(table, memory, w_key, w_value):
    slots, depth = memory.shape[0], memory.shape[2]
    dma = pltpu.SemaphoreType.DMA
    vmem, smem, anywhere = (pl.BlockSpec(memory_space=s) for s in (pltpu.VMEM, pltpu.SMEM, pl.ANY))
    return pl.pallas_call(
        move_kernel,
        out_shape=(
            jax.ShapeDtypeStruct((NDP * RM, 512), BF16),
            jax.ShapeDtypeStruct((NDP, RK, 512), BF16),
            jax.ShapeDtypeStruct((NDP, 8, 128), jnp.int32),
        ),
        in_specs=[smem, anywhere, anywhere, anywhere],
        out_specs=(vmem, vmem, vmem),
        scratch_shapes=[
            pltpu.VMEM((slots, RM, 256), BF16),
            pltpu.VMEM((slots, RK, depth), BF16),
            pltpu.VMEM((slots, RK, 512), BF16),
            pltpu.VMEM((depth, 512), BF16),
            pltpu.VMEM((NDP, RM, 256), BF16),
            pltpu.VMEM((NDP, RK, 512), BF16),
            pltpu.VMEM((NDP, 8, 128), jnp.int32),
            pltpu.VMEM((NHEAD, NDP * RM, 256), BF16),
            dma((4,)),
            *[dma((NDP,)) for _ in range(6)],
            *[dma((NGROUP,)) for _ in range(6)],
            dma((4, NGROUP)),
            dma((4, NGROUP)),
        ],
        compiler_params=pltpu.CompilerParams(
            collective_id=0, has_side_effects=True, vmem_limit_bytes=56 * 2**20
        ),
        cost_estimate=pl.CostEstimate(
            flops=2 * NDP * BLOCK * depth * 512, bytes_accessed=24 * 2**20, transcendentals=0
        ),
        name="move",
    )(table, memory, w_key, w_value)


def attend_kernel(where_of, lengths, kv_mem, kv_dir, query, w_out, keys, values, partial, score, att, ctx):
    requests = query.shape[0]
    span = MAXB * BLOCK
    for r in range(requests):
        for b in range(MAXB):
            k = where_of[r * MAXB + b]
            used = lengths[r] > b * BLOCK
            high = kv_mem[pl.ds(pl.multiple_of(k * RM, 16), RM), :]
            low = kv_dir[k]
            high = jnp.where(used, high, jnp.zeros_like(high))
            low = jnp.where(used, low, jnp.zeros_like(low))
            keys[r, b * BLOCK : b * BLOCK + RM, :] = high[:, 0:256]
            keys[r, b * BLOCK + RM : (b + 1) * BLOCK, :] = low[:, 0:256]
            values[r, b * BLOCK : b * BLOCK + RM, :] = high[:, 256:512]
            values[r, b * BLOCK + RM : (b + 1) * BLOCK, :] = low[:, 256:512]
    own_head = lax.broadcasted_iota(jnp.int32, (8, 256), 1) // HEAD_DIM == lax.broadcasted_iota(
        jnp.int32, (8, 256), 0
    )
    for r in range(requests):
        spread = jnp.where(own_head, jnp.broadcast_to(query[r : r + 1, :].astype(jnp.float32), (8, 256)), 0.0)
        dots = lax.dot_general(
            spread.astype(BF16), keys[r], (((1,), (1,)), ((), ())), preferred_element_type=jnp.float32
        )
        position = lax.broadcasted_iota(jnp.int32, (8, span), 1)
        score[r * 8 : (r + 1) * 8, :] = jnp.where(position < lengths[r], dots, -1e30)
    scores = score[...]
    expo = jnp.exp(scores - jnp.max(scores, axis=1, keepdims=True))
    att[...] = (expo / jnp.sum(expo, axis=1, keepdims=True)).astype(BF16)
    ctx[...] = jnp.zeros_like(ctx)
    for r in range(requests):
        mixed = jnp.dot(att[r * 8 : (r + 1) * 8, :], values[r], preferred_element_type=jnp.float32)
        ctx[r : r + 1, :] = jnp.sum(jnp.where(own_head, mixed, 0.0), axis=0, keepdims=True)
    summed = jnp.dot(ctx[...].astype(BF16), w_out[...], preferred_element_type=jnp.float32)
    for p in range(NHEAD):
        partial[p] = summed[:, p * 256 : (p + 1) * 256]


def attend(where_of, lengths, kv_mem, kv_dir, query, w_out):
    requests = query.shape[0]
    span = MAXB * BLOCK
    vmem, smem = (pl.BlockSpec(memory_space=s) for s in (pltpu.VMEM, pltpu.SMEM))
    return pl.pallas_call(
        attend_kernel,
        out_shape=(
            jax.ShapeDtypeStruct((requests, span, 256), BF16),
            jax.ShapeDtypeStruct((requests, span, 256), BF16),
            jax.ShapeDtypeStruct((NHEAD, 8, 256), jnp.float32),
        ),
        in_specs=[smem, smem, vmem, vmem, vmem, vmem],
        out_specs=(vmem, vmem, vmem),
        scratch_shapes=[
            pltpu.VMEM((requests * 8, span), jnp.float32),
            pltpu.VMEM((requests * 8, span), BF16),
            pltpu.VMEM((8, 256), jnp.float32),
        ],
        compiler_params=pltpu.CompilerParams(vmem_limit_bytes=40 * 2**20),
        name="attend",
    )(where_of, lengths, kv_mem, kv_dir, query, w_out)


def sum_kernel(partial, hidden, out, parts, send, recv):
    dp, head = lax.axis_index("dp"), lax.axis_index("head")
    barrier = pltpu.get_barrier_semaphore()
    for step in range(1, NHEAD):
        other = (head + step) % NHEAD
        pl.semaphore_signal(barrier, inc=1, device_id=(dp, other), device_id_type=MESH)
    pl.semaphore_wait(barrier, NHEAD - 1)
    copies = []
    for step in range(1, NHEAD):
        other = (head + step) % NHEAD
        copy = pltpu.make_async_remote_copy(
            src_ref=partial.at[other], dst_ref=parts.at[step], send_sem=send.at[step], recv_sem=recv.at[step],
            device_id=(dp, other), device_id_type=MESH)
        copy.start()
        copies.append(copy)
    total = partial[head]
    for step, copy in enumerate(copies, 1):
        copy.wait_recv()
        total = total + parts[step]
    requests = hidden.shape[0]
    out[...] = (hidden[...].astype(jnp.float32) + total[0:requests, :]).astype(BF16)
    for copy in copies:
        copy.wait_send()


def sum_heads(partial, hidden):
    vmem = pl.BlockSpec(memory_space=pltpu.VMEM)
    return pl.pallas_call(
        sum_kernel,
        out_shape=jax.ShapeDtypeStruct(hidden.shape, BF16),
        in_specs=[vmem, vmem],
        out_specs=vmem,
        scratch_shapes=[
            pltpu.VMEM((NHEAD, 8, 256), jnp.float32),
            pltpu.SemaphoreType.DMA((NHEAD,)),
            pltpu.SemaphoreType.DMA((NHEAD,)),
        ],
        compiler_params=pltpu.CompilerParams(collective_id=1, has_side_effects=True),
        name="sum_heads",
    )(partial, hidden)


def shards(memory, block_route, enc_len, w_key, w_value, dec_query, dec_hidden, w_out):
    slots = block_route.shape[1]
    cells = enc_len.shape[0] * MAXB
    to_home = block_route[0][None, :] == jnp.arange(NDP)[:, None]
    index = jnp.sum(jnp.where(to_home, jnp.arange(slots)[None, :], 0), axis=1)
    cell = jnp.sum(jnp.where(to_home, block_route[1][None, :] + 1, 0), axis=1) - 1
    table = jnp.stack([index, cell]).astype(jnp.int32)
    blocks = memory.reshape(slots, BLOCK, memory.shape[1])
    kv_mem, kv_dir, tags = move(table, blocks, w_key, w_value)
    from_slot = tags[:, 0, 0][None, :] == jnp.arange(cells)[:, None]
    where_of = jnp.sum(jnp.where(from_slot, jnp.arange(NDP)[None, :], 0), axis=1).astype(jnp.int32)
    keys, values, partial = attend(where_of, enc_len, kv_mem, kv_dir, dec_query, w_out)
    new_hidden = sum_heads(partial, dec_hidden)
    return new_hidden, keys, values


def solution(mesh):
    in_specs = (
        P("dp", None),
        P(None, "dp"),
        P("dp"),
        P(None, "head"),
        P(None, "head"),
        P("dp", "head"),
        P("dp", "head"),
        P("head", None),
    )
    out_specs = (P("dp", "head"), P("dp", None, "head"), P("dp", None, "head"))
    return jax.shard_map(shards, mesh=mesh, in_specs=in_specs, out_specs=out_specs, check_vma=False)
```

```python
import functools

import jax
import jax.numpy as jnp
from jax import lax
from jax.experimental import pallas as pl
from jax.experimental.pallas import tpu as pltpu
from jax.sharding import PartitionSpec as P

HEAD_DIM = 64
BLOCK = 128
MAXB = 4
ZN, YN, XN, CN = 8, 4, 4, 2
NDP, NHEAD = ZN * YN, XN * CN
COLS = 256
DIRECT = 10
GROUP = 2
LAG = 1
NMEM = NDP - DIRECT
NGROUP = NMEM // GROUP
MESH = pl.DeviceIdType.MESH
BF16 = jnp.bfloat16
F32 = jnp.float32


def slot_offset(k):
    outer = (k + NDP - YN) // NDP
    last = k // (NDP - YN)
    middle = outer - last
    m = (k + NDP - YN) % NDP
    dz = middle * (m // 8 + 1) * (1 - 2 * (m % 2)) + last * (ZN // 2) + ZN
    j = (1 - outer) * k + middle * ((m % 8) // 2) + last * (k - NDP + YN)
    dy = (j % 2) * ((j + 1) // 2) + (1 - j % 2) * (YN - j // 2)
    return dz, dy


def each(first, last, act):
    def step(k, _):
        act(k)
        return 0

    lax.fori_loop(first, last, step, 0)


def whole_kernel(
    route, lengths, query, hidden, mem, wk, wv, wo, new_hidden, keys, values,
    own, full, wts, wout, packed, kv_out, tag_out, tags, place, pool, kv, key_grid, value_grid,
    score, att, ctx, partial, parts, home_of, cells,
    in_sem, a_send, a_recv, d_send, d_recv, t_send, t_recv,
    xp_send, xp_recv, xm_send, xm_recv, f_send, f_recv, c_send, c_recv, s_send, s_recv, out_sem,
):
    dp, head = lax.axis_index("dp"), lax.axis_index("head")
    z, y = dp // YN, dp % YN
    x, core = head // CN, head % CN
    right = ((x + 1) % XN) * CN + core
    left = ((x + XN - 1) % XN) * CN + core
    across = ((x + 2) % XN) * CN + core
    twin = x * CN + 1 - core
    slots = mem.shape[0]
    requests = query.shape[0]

    def peer(k):
        dz, dy = slot_offset(k)
        return ((z + dz) % ZN) * YN + (y + dy) % YN

    columns = pl.ds(pl.multiple_of(head * COLS, COLS), COLS)
    loads = [
        pltpu.make_async_copy(mem.at[:, :, columns], own, in_sem.at[0]),
        pltpu.make_async_copy(mem, full, in_sem.at[1]),
        pltpu.make_async_copy(wk, wts.at[:, 0:COLS], in_sem.at[2]),
        pltpu.make_async_copy(wv, wts.at[:, COLS : 2 * COLS], in_sem.at[3]),
        pltpu.make_async_copy(wo, wout, in_sem.at[4]),
    ]
    for load in loads:
        load.start()

    barrier = pltpu.get_barrier_semaphore()

    def greet(k):
        pl.semaphore_signal(barrier, inc=1, device_id=(peer(k), head), device_id_type=MESH)

    each(1, NDP, greet)
    for step in range(1, NHEAD):
        pl.semaphore_signal(barrier, inc=1, device_id=(dp, (head + step) % NHEAD), device_id_type=MESH)

    to_home = [route[0, j] for j in range(slots)]

    def look_up(k):
        home = peer(k)
        index, cell = jnp.int32(0), jnp.int32(-1)
        for j in range(slots):
            hit = to_home[j] == home
            index = jnp.where(hit, j, index)
            cell = jnp.where(hit, route[1, j], cell)
        home_of[k] = index
        tag_out[k] = jnp.full((1, 128), cell, jnp.int32)

    each(0, NDP, look_up)
    tags[0] = tag_out[0]

    loads[0].wait()

    def fill(k):
        packed[k - DIRECT] = own[home_of[k]]

    each(DIRECT, NDP, fill)
    pl.semaphore_wait(barrier, NDP - 1 + NHEAD - 1)

    def rows_of(g):
        return pl.ds(pl.multiple_of(g * (GROUP * BLOCK), GROUP * BLOCK), GROUP * BLOCK)

    def a_copy(k):
        rows = pl.ds(pl.multiple_of((k - DIRECT) * BLOCK, BLOCK), BLOCK)
        return pltpu.make_async_remote_copy(
            src_ref=packed.at[k - DIRECT], dst_ref=pool.at[head, rows, :],
            send_sem=a_send.at[k], recv_sem=a_recv.at[k],
            device_id=(peer(k), head), device_id_type=MESH)

    def t_copy(k):
        return pltpu.make_async_remote_copy(
            src_ref=tag_out.at[k], dst_ref=tags.at[k],
            send_sem=t_send.at[k], recv_sem=t_recv.at[k],
            device_id=(peer(k), head), device_id_type=MESH)

    def d_copy(k):
        return pltpu.make_async_remote_copy(
            src_ref=kv_out.at[k], dst_ref=kv.at[k],
            send_sem=d_send.at[k], recv_sem=d_recv.at[k],
            device_id=(peer(k), head), device_id_type=MESH)

    each(DIRECT, NDP, lambda k: a_copy(k).start())

    def project(rows):
        return jnp.dot(rows, wts[...], preferred_element_type=F32).astype(BF16)

    for load in loads[1:4]:
        load.wait()

    def direct_group(g):
        base = g * GROUP
        rows = jnp.concatenate([full[home_of[base + i]] for i in range(GROUP)], axis=0)
        kv_out[pl.ds(base, GROUP)] = project(rows).reshape(GROUP, BLOCK, 2 * COLS)
        for i in range(GROUP):
            pl.when(base + i > 0)(lambda k=base + i: d_copy(k).start())

    each(0, DIRECT // GROUP, direct_group)
    kv[0] = kv_out[0]
    each(1, NDP, lambda k: t_copy(k).start())

    def head_copy(piece, group, target, send, recv):
        where = pool.at[piece, rows_of(group), :]
        return pltpu.make_async_remote_copy(
            src_ref=where, dst_ref=where, send_sem=send, recv_sem=recv,
            device_id=(dp, target), device_id_type=MESH)

    def plus_copy(g):
        return head_copy(head, g, right, xp_send.at[g], xp_recv.at[g])

    def minus_copy(g):
        return head_copy(head, g, left, xm_send.at[g], xm_recv.at[g])

    def forward_right(g):
        return head_copy(left, g, right, f_send.at[g], f_recv.at[g])

    def forward_left(g):
        return head_copy(right, g, left, f_send.at[g], f_recv.at[g])

    def core_copy(piece, n, g):
        return head_copy(piece, g, twin, c_send.at[n, g], c_recv.at[n, g])

    def stage_own(g):
        each(DIRECT + g * GROUP, DIRECT + (g + 1) * GROUP, lambda k: a_copy(k).wait_recv())
        plus_copy(g).start()
        minus_copy(g).start()
        core_copy(head, 0, g).start()

    def stage_forward(g):
        plus_copy(g).wait_recv()
        minus_copy(g).wait_recv()
        pl.when(g % 2 == 0)(lambda: forward_right(g).start())
        pl.when(g % 2 == 1)(lambda: forward_left(g).start())
        core_copy(left, 1, g).start()
        core_copy(right, 2, g).start()

    def stage_core(g):
        forward_right(g).wait_recv()
        core_copy(across, 3, g).start()

    def stage_project(g):
        for n in range(4):
            core_copy(head, n, g).wait_recv()
        rows = jnp.concatenate([pool[p, rows_of(g), :] for p in range(NHEAD)], axis=1)
        kv[pl.ds(DIRECT + g * GROUP, GROUP)] = project(rows).reshape(GROUP, BLOCK, 2 * COLS)

    def round_of(t):
        for late, stage in enumerate((stage_own, stage_forward, stage_core, stage_project)):
            g = t - late * LAG
            pl.when((g >= 0) & (g < NGROUP))(functools.partial(stage, g))

    each(0, NGROUP + 2 * LAG, round_of)

    each(1, NDP, lambda k: t_copy(k).wait_recv())
    lane = lax.broadcasted_iota(jnp.int32, (NDP, 1, 128), 2)
    slot = lax.broadcasted_iota(jnp.int32, (NDP, 1, 128), 0)
    place[...] = jnp.max(jnp.where(tags[...] == lane, slot, 0), axis=0)
    to_scalars = pltpu.make_async_copy(place, cells, in_sem.at[5])
    to_scalars.start()

    each(NGROUP + 2 * LAG, NGROUP + 3 * LAG, round_of)
    each(1, DIRECT, lambda k: d_copy(k).wait_recv())
    to_scalars.wait()

    span = MAXB * BLOCK
    outs = []
    for r in range(requests):
        for b in range(MAXB):
            block = kv[cells[0, r * MAXB + b]]
            block = jnp.where(lengths[r] > b * BLOCK, block, jnp.zeros_like(block))
            key_grid[r, b * BLOCK : (b + 1) * BLOCK, :] = block[:, 0:COLS]
            value_grid[r, b * BLOCK : (b + 1) * BLOCK, :] = block[:, COLS : 2 * COLS]
        outs.append(pltpu.make_async_copy(key_grid.at[r], keys.at[r], out_sem.at[0, r]))
        outs.append(pltpu.make_async_copy(value_grid.at[r], values.at[r], out_sem.at[1, r]))
        for copy in outs[-2:]:
            copy.start()

    own_head = lax.broadcasted_iota(jnp.int32, (8, COLS), 1) // HEAD_DIM == lax.broadcasted_iota(
        jnp.int32, (8, COLS), 0
    )
    position = lax.broadcasted_iota(jnp.int32, (8, span), 1)
    for r in range(requests):
        spread = jnp.where(own_head, jnp.broadcast_to(query[r : r + 1, :].astype(F32), (8, COLS)), 0.0)
        dots = lax.dot_general(
            spread.astype(BF16), key_grid[r], (((1,), (1,)), ((), ())), preferred_element_type=F32
        )
        score[r * 8 : (r + 1) * 8, :] = jnp.where(position < lengths[r], dots, -1e30)
    scores = score[...]
    expo = jnp.exp(scores - jnp.max(scores, axis=1, keepdims=True))
    att[...] = (expo / jnp.sum(expo, axis=1, keepdims=True)).astype(BF16)
    ctx[...] = jnp.zeros_like(ctx)
    for r in range(requests):
        mixed = jnp.dot(att[r * 8 : (r + 1) * 8, :], value_grid[r], preferred_element_type=F32)
        ctx[r : r + 1, :] = jnp.sum(jnp.where(own_head, mixed, 0.0), axis=0, keepdims=True)
    loads[4].wait()
    summed = jnp.dot(ctx[...].astype(BF16), wout[...], preferred_element_type=F32)
    for p in range(NHEAD):
        partial[p] = summed[:, p * COLS : (p + 1) * COLS]

    def s_copy(step):
        other = (head + step) % NHEAD
        return pltpu.make_async_remote_copy(
            src_ref=partial.at[other], dst_ref=parts.at[step],
            send_sem=s_send.at[step], recv_sem=s_recv.at[step],
            device_id=(dp, other), device_id_type=MESH)

    for step in range(1, NHEAD):
        s_copy(step).start()

    each(DIRECT, NDP, lambda k: a_copy(k).wait_send())
    each(1, DIRECT, lambda k: d_copy(k).wait_send())
    each(1, NDP, lambda k: t_copy(k).wait_send())

    def settle_group(g):
        plus_copy(g).wait_send()
        minus_copy(g).wait_send()
        forward_right(g).wait_send()
        for n in range(4):
            core_copy(head, n, g).wait_send()

    each(0, NGROUP, settle_group)

    total = partial[head]
    for step in range(1, NHEAD):
        s_copy(step).wait_recv()
        total = total + parts[step]
    new_hidden[...] = (hidden[...].astype(F32) + total[0:requests, :]).astype(BF16)
    for step in range(1, NHEAD):
        s_copy(step).wait_send()
    for copy in outs:
        copy.wait()


def shards(memory, block_route, enc_len, w_key, w_value, dec_query, dec_hidden, w_out):
    slots, depth, requests = block_route.shape[1], memory.shape[1], enc_len.shape[0]
    span = MAXB * BLOCK
    dma, bufs = pltpu.SemaphoreType.DMA, pltpu.VMEM
    vmem, smem, anywhere = (pl.BlockSpec(memory_space=s) for s in (pltpu.VMEM, pltpu.SMEM, pl.ANY))
    grid = jax.ShapeDtypeStruct((requests, span, COLS), BF16)
    return pl.pallas_call(
        whole_kernel,
        out_shape=(jax.ShapeDtypeStruct(dec_hidden.shape, BF16), grid, grid),
        in_specs=[smem, smem, vmem, vmem, anywhere, anywhere, anywhere, anywhere],
        out_specs=(vmem, anywhere, anywhere),
        scratch_shapes=[
            bufs((slots, BLOCK, COLS), BF16),
            bufs((slots, BLOCK, depth), BF16),
            bufs((depth, 2 * COLS), BF16),
            bufs((COLS, depth), BF16),
            bufs((NMEM, BLOCK, COLS), BF16),
            bufs((DIRECT, BLOCK, 2 * COLS), BF16),
            bufs((NDP, 1, 128), jnp.int32),
            bufs((NDP, 1, 128), jnp.int32),
            bufs((1, 128), jnp.int32),
            bufs((NHEAD, NMEM * BLOCK, COLS), BF16),
            bufs((NDP, BLOCK, 2 * COLS), BF16),
            bufs((requests, span, COLS), BF16),
            bufs((requests, span, COLS), BF16),
            bufs((requests * 8, span), F32),
            bufs((requests * 8, span), BF16),
            bufs((8, COLS), F32),
            bufs((NHEAD, 8, COLS), F32),
            bufs((NHEAD, 8, COLS), F32),
            pltpu.SMEM((NDP,), jnp.int32),
            pltpu.SMEM((1, 128), jnp.int32),
            dma((6,)),
            *[dma((NDP,)) for _ in range(6)],
            *[dma((NGROUP,)) for _ in range(6)],
            dma((4, NGROUP)),
            dma((4, NGROUP)),
            dma((NHEAD,)),
            dma((NHEAD,)),
            dma((2, requests)),
        ],
        compiler_params=pltpu.CompilerParams(
            collective_id=0, has_side_effects=True, vmem_limit_bytes=56 * 2**20
        ),
        cost_estimate=pl.CostEstimate(
            flops=2 * NDP * BLOCK * depth * 2 * COLS, bytes_accessed=24 * 2**20, transcendentals=0
        ),
        name="whole",
    )(block_route, enc_len, dec_query, dec_hidden, memory.reshape(slots, BLOCK, depth), w_key, w_value, w_out)


def solution(mesh):
    in_specs = (
        P("dp", None),
        P(None, "dp"),
        P("dp"),
        P(None, "head"),
        P(None, "head"),
        P("dp", "head"),
        P("dp", "head"),
        P("head", None),
    )
    out_specs = (P("dp", "head"), P("dp", None, "head"), P("dp", None, "head"))
    return jax.shard_map(shards, mesh=mesh, in_specs=in_specs, out_specs=out_specs, check_vma=False)
```

```python
import functools

import jax
import jax.numpy as jnp
from jax import lax
from jax.experimental import pallas as pl
from jax.experimental.pallas import tpu as pltpu
from jax.sharding import PartitionSpec as P

HEAD_DIM = 64
BLOCK = 128
MAXB = 4
ZN, YN, XN, CN = 8, 4, 4, 2
NDP, NHEAD = ZN * YN, XN * CN
COLS = 256
DIRECT = 10
GROUP = 2
LAG = 1

EARLY = 3
NMEM = NDP - DIRECT
NGROUP = NMEM // GROUP
MESH = pl.DeviceIdType.MESH
BF16 = jnp.bfloat16
F32 = jnp.float32


def slot_offset(k):
    outer = (k + NDP - YN) // NDP
    last = k // (NDP - YN)
    middle = outer - last
    m = (k + NDP - YN) % NDP
    dz = middle * (m // 8 + 1) * (1 - 2 * (m % 2)) + last * (ZN // 2) + ZN
    j = (1 - outer) * k + middle * ((m % 8) // 2) + last * (k - NDP + YN)
    turn = 1 - 2 * middle * (m % 2)
    dy = turn * ((j % 2) * ((j + 1) // 2) - (1 - j % 2) * (j // 2)) + YN
    return dz, dy


def each(first, last, act):
    def step(k, _):
        act(k)
        return 0

    lax.fori_loop(first, last, step, 0)


def whole_kernel(
    route_in, lengths_in, query_in, hidden_in, mem, wk, wv, wo, new_hidden, keys, values,
    own, full, wts, wout, packed, kv_out, tag_out, tags, place, pool, kv, key_grid, value_grid,
    score, att, ctx, partial, parts, home_of, cells, route, lengths, query, hidden, summed_hidden,
    in_sem, a_send, a_recv, d_send, d_recv, t_send, t_recv,
    xp_send, xp_recv, xm_send, xm_recv, f_send, f_recv, c_send, c_recv, s_send, s_recv, out_sem,
):
    dp, head = lax.axis_index("dp"), lax.axis_index("head")
    z, y = lax.div(dp, YN), lax.rem(dp, YN)
    x, core = lax.div(head, CN), lax.rem(head, CN)
    right = lax.rem(x + 1, XN) * CN + core
    left = lax.rem(x + XN - 1, XN) * CN + core
    across = lax.rem(x + 2, XN) * CN + core
    twin = x * CN + 1 - core
    slots = mem.shape[0]
    requests = keys.shape[0]

    def peer(k):
        dz, dy = slot_offset(k)
        return lax.rem(z + dz, ZN) * YN + lax.rem(y + dy, YN)

    columns = pl.ds(pl.multiple_of(head * COLS, COLS), COLS)
    get_route = pltpu.make_async_copy(route_in, route, in_sem.at[6])
    get_route.start()
    loads = [
        pltpu.make_async_copy(mem.at[:, :, columns], own, in_sem.at[0]),
        pltpu.make_async_copy(mem, full, in_sem.at[1]),
        pltpu.make_async_copy(wk, wts.at[:, 0:COLS], in_sem.at[2]),
        pltpu.make_async_copy(wv, wts.at[:, COLS : 2 * COLS], in_sem.at[3]),
        pltpu.make_async_copy(wo, wout, in_sem.at[4]),
        pltpu.make_async_copy(lengths_in, lengths, in_sem.at[7]),
        pltpu.make_async_copy(query_in, query, in_sem.at[8]),
        pltpu.make_async_copy(hidden_in, hidden, in_sem.at[9]),
    ]
    for load in loads:
        load.start()

    barrier = pltpu.get_barrier_semaphore()

    for k in range(NDP - 1, 0, -1):
        pl.semaphore_signal(barrier, inc=1, device_id=(peer(k), head), device_id_type=MESH)
    for step in range(1, NHEAD):
        pl.semaphore_signal(barrier, inc=1, device_id=(dp, lax.rem(head + step, NHEAD)), device_id_type=MESH)

    get_route.wait()
    to_home = [route[0, j] for j in range(slots)]

    for k in range(NDP):
        home = peer(k)
        index = jnp.int32(0)
        for j in range(slots):
            index = jnp.where(to_home[j] == home, j, index)
        home_of[k] = index

    loads[0].wait()

    for k in range(DIRECT, NDP):
        packed[k - DIRECT] = own[home_of[k]]
    pl.semaphore_wait(barrier, NDP - 1 + NHEAD - 1)

    def rows_of(g):
        return pl.ds(pl.multiple_of(g * (GROUP * BLOCK), GROUP * BLOCK), GROUP * BLOCK)

    def a_copy(k):
        rows = pl.ds(pl.multiple_of((k - DIRECT) * BLOCK, BLOCK), BLOCK)
        return pltpu.make_async_remote_copy(
            src_ref=packed.at[k - DIRECT], dst_ref=pool.at[head, rows, :],
            send_sem=a_send.at[k], recv_sem=a_recv.at[k],
            device_id=(peer(k), head), device_id_type=MESH)

    def t_copy(k):
        return pltpu.make_async_remote_copy(
            src_ref=tag_out.at[k], dst_ref=tags.at[k],
            send_sem=t_send.at[k], recv_sem=t_recv.at[k],
            device_id=(peer(k), head), device_id_type=MESH)

    def d_copy(k):
        return pltpu.make_async_remote_copy(
            src_ref=kv_out.at[k], dst_ref=kv.at[k],
            send_sem=d_send.at[k], recv_sem=d_recv.at[k],
            device_id=(peer(k), head), device_id_type=MESH)

    for k in range(DIRECT, NDP):
        a_copy(k).start()

    rows_k = lax.broadcasted_iota(jnp.int32, (NDP, 1, 128), 0)
    offset_z, offset_y = slot_offset(rows_k)
    homes = ((z + offset_z) % ZN) * YN + (y + offset_y) % YN
    cell = jnp.full((NDP, 1, 128), -1, jnp.int32)
    for j in range(slots):
        cell = jnp.where(homes == to_home[j], route[1, j], cell)
    tag_out[...] = cell
    tags[0] = cell[0]
    for k in range(1, NDP):
        t_copy(k).start()

    def project(rows):
        return jnp.dot(rows, wts[...], preferred_element_type=F32).astype(BF16)

    def direct_group(g):
        base = g * GROUP
        rows = jnp.concatenate([full[home_of[base + i]] for i in range(GROUP)], axis=0)
        kv_out[pl.ds(base, GROUP)] = project(rows).reshape(GROUP, BLOCK, 2 * COLS)
        for i in range(GROUP):
            pl.when(base + i > 0)(lambda k=base + i: d_copy(k).start())

    def head_copy(piece, group, target, send, recv):
        where = pool.at[piece, rows_of(group), :]
        return pltpu.make_async_remote_copy(
            src_ref=where, dst_ref=where, send_sem=send, recv_sem=recv,
            device_id=(dp, target), device_id_type=MESH)

    def plus_copy(g):
        return head_copy(head, g, right, xp_send.at[g], xp_recv.at[g])

    def minus_copy(g):
        return head_copy(head, g, left, xm_send.at[g], xm_recv.at[g])

    def forward_right(g):
        return head_copy(left, g, right, f_send.at[g], f_recv.at[g])

    def forward_left(g):
        return head_copy(right, g, left, f_send.at[g], f_recv.at[g])

    def core_copy(piece, n, g):
        return head_copy(piece, g, twin, c_send.at[n, g], c_recv.at[n, g])

    def stage_own(g):
        each(DIRECT + g * GROUP, DIRECT + (g + 1) * GROUP, lambda k: a_copy(k).wait_recv())
        plus_copy(g).start()
        minus_copy(g).start()
        core_copy(head, 0, g).start()

    def stage_forward(g):
        plus_copy(g).wait_recv()
        minus_copy(g).wait_recv()
        pl.when(g % 2 == 0)(lambda: forward_right(g).start())
        pl.when(g % 2 == 1)(lambda: forward_left(g).start())
        core_copy(left, 1, g).start()
        core_copy(right, 2, g).start()

    def stage_core(g):
        forward_right(g).wait_recv()
        core_copy(across, 3, g).start()

    def stage_project(g):
        for n in range(4):
            core_copy(head, n, g).wait_recv()
        rows = jnp.concatenate([pool[p, rows_of(g), :] for p in range(NHEAD)], axis=1)
        kv[pl.ds(DIRECT + g * GROUP, GROUP)] = project(rows).reshape(GROUP, BLOCK, 2 * COLS)

    def round_of(t):
        def weights():
            for load in loads[1:]:
                load.wait()

        pl.when(t == EARLY)(weights)
        for late, stage in enumerate((stage_own, stage_forward, stage_core, stage_project)):
            g = t - late * LAG
            pl.when((g >= 0) & (g < NGROUP))(functools.partial(stage, g))
        n = t - EARLY
        pl.when((n >= 0) & (n < DIRECT // GROUP))(lambda: direct_group(n))

    each(0, NGROUP + 2 * LAG, round_of)

    each(1, NDP, lambda k: t_copy(k).wait_recv())
    lane = lax.broadcasted_iota(jnp.int32, (NDP, 1, 128), 2)
    slot = lax.broadcasted_iota(jnp.int32, (NDP, 1, 128), 0)
    place[...] = jnp.max(jnp.where(tags[...] == lane, slot, 0), axis=0)
    to_scalars = pltpu.make_async_copy(place, cells, in_sem.at[5])
    to_scalars.start()

    each(NGROUP + 2 * LAG, NGROUP + 3 * LAG, round_of)
    kv[0] = kv_out[0]
    each(1, DIRECT, lambda k: d_copy(k).wait_recv())
    to_scalars.wait()

    span = MAXB * BLOCK
    outs = []
    for r in range(requests):
        for b in range(MAXB):
            block = kv[cells[0, r * MAXB + b]]
            block = jnp.where(lengths[r] > b * BLOCK, block, jnp.zeros_like(block))
            key_grid[r, b * BLOCK : (b + 1) * BLOCK, :] = block[:, 0:COLS]
            value_grid[r, b * BLOCK : (b + 1) * BLOCK, :] = block[:, COLS : 2 * COLS]
        outs.append(pltpu.make_async_copy(key_grid.at[r], keys.at[r], out_sem.at[0, r]))
        outs.append(pltpu.make_async_copy(value_grid.at[r], values.at[r], out_sem.at[1, r]))
        for copy in outs[-2:]:
            copy.start()

    own_head = lax.broadcasted_iota(jnp.int32, (8, COLS), 1) // HEAD_DIM == lax.broadcasted_iota(
        jnp.int32, (8, COLS), 0
    )
    position = lax.broadcasted_iota(jnp.int32, (8, span), 1)
    for r in range(requests):
        spread = jnp.where(own_head, jnp.broadcast_to(query[r : r + 1, :].astype(F32), (8, COLS)), 0.0)
        dots = lax.dot_general(
            spread.astype(BF16), key_grid[r], (((1,), (1,)), ((), ())), preferred_element_type=F32
        )
        score[r * 8 : (r + 1) * 8, :] = jnp.where(position < lengths[r], dots, -1e30)
    scores = score[...]
    expo = jnp.exp(scores - jnp.max(scores, axis=1, keepdims=True))
    att[...] = (expo / jnp.sum(expo, axis=1, keepdims=True)).astype(BF16)
    ctx[...] = jnp.zeros_like(ctx)
    for r in range(requests):
        mixed = jnp.dot(att[r * 8 : (r + 1) * 8, :], value_grid[r], preferred_element_type=F32)
        ctx[r : r + 1, :] = jnp.sum(jnp.where(own_head, mixed, 0.0), axis=0, keepdims=True)
    summed = jnp.dot(ctx[...].astype(BF16), wout[...], preferred_element_type=F32)
    for p in range(NHEAD):
        partial[p] = summed[:, p * COLS : (p + 1) * COLS]

    def s_copy(step):
        other = lax.rem(head + step, NHEAD)
        return pltpu.make_async_remote_copy(
            src_ref=partial.at[other], dst_ref=parts.at[step],
            send_sem=s_send.at[step], recv_sem=s_recv.at[step],
            device_id=(dp, other), device_id_type=MESH)

    for step in range(1, NHEAD):
        s_copy(step).start()

    each(DIRECT, NDP, lambda k: a_copy(k).wait_send())
    each(1, DIRECT, lambda k: d_copy(k).wait_send())
    each(1, NDP, lambda k: t_copy(k).wait_send())

    def settle_group(g):
        plus_copy(g).wait_send()
        minus_copy(g).wait_send()
        forward_right(g).wait_send()
        for n in range(4):
            core_copy(head, n, g).wait_send()

    each(0, NGROUP, settle_group)

    total = partial[head]
    for step in range(1, NHEAD):
        s_copy(step).wait_recv()
        total = total + parts[step]
    summed_hidden[...] = (hidden[...].astype(F32) + total[0:requests, :]).astype(BF16)
    outs.append(pltpu.make_async_copy(summed_hidden, new_hidden, in_sem.at[10]))
    outs[-1].start()
    for step in range(1, NHEAD):
        s_copy(step).wait_send()
    for copy in outs:
        copy.wait()


def hand_on_kernel(hidden_in, keys_in, values_in, hidden, keys, values, staged, small, in_sem, out_sem, small_sem):
    requests = keys.shape[0]
    steps = [(i, r) for r in range(requests) for i in range(2)]
    takes, gives = [], []
    for i, r in steps:
        source, target = (keys_in, keys) if i == 0 else (values_in, values)
        takes.append(pltpu.make_async_copy(source.at[r], staged.at[i, r], in_sem.at[i, r]))
        gives.append(pltpu.make_async_copy(staged.at[i, r], target.at[r], out_sem.at[i, r]))
    get_small = pltpu.make_async_copy(hidden_in, small, small_sem.at[0])
    put_small = pltpu.make_async_copy(small, hidden, small_sem.at[1])
    get_small.start()
    for take in takes:
        take.start()
    get_small.wait()
    put_small.start()
    for take, give in zip(takes, gives):
        take.wait()
        give.start()
    for give in gives:
        give.wait()
    put_small.wait()


def shards(memory, block_route, enc_len, w_key, w_value, dec_query, dec_hidden, w_out):
    slots, depth, requests = block_route.shape[1], memory.shape[1], enc_len.shape[0]
    span = MAXB * BLOCK
    dma, bufs = pltpu.SemaphoreType.DMA, pltpu.VMEM
    anywhere = pl.BlockSpec(memory_space=pl.ANY)
    grid = jax.ShapeDtypeStruct((requests, span, COLS), BF16)
    results = pl.pallas_call(
        whole_kernel,
        out_shape=(jax.ShapeDtypeStruct(dec_hidden.shape, BF16), grid, grid),
        in_specs=[anywhere] * 8,
        out_specs=(anywhere, anywhere, anywhere),
        scratch_shapes=[
            bufs((slots, BLOCK, COLS), BF16),
            bufs((slots, BLOCK, depth), BF16),
            bufs((depth, 2 * COLS), BF16),
            bufs((COLS, depth), BF16),
            bufs((NMEM, BLOCK, COLS), BF16),
            bufs((DIRECT, BLOCK, 2 * COLS), BF16),
            bufs((NDP, 1, 128), jnp.int32),
            bufs((NDP, 1, 128), jnp.int32),
            bufs((1, 128), jnp.int32),
            bufs((NHEAD, NMEM * BLOCK, COLS), BF16),
            bufs((NDP, BLOCK, 2 * COLS), BF16),
            bufs((requests, span, COLS), BF16),
            bufs((requests, span, COLS), BF16),
            bufs((requests * 8, span), F32),
            bufs((requests * 8, span), BF16),
            bufs((8, COLS), F32),
            bufs((NHEAD, 8, COLS), F32),
            bufs((NHEAD, 8, COLS), F32),
            pltpu.SMEM((NDP,), jnp.int32),
            pltpu.SMEM((1, 128), jnp.int32),
            pltpu.SMEM(block_route.shape, jnp.int32),
            pltpu.SMEM(enc_len.shape, jnp.int32),
            bufs(dec_query.shape, BF16),
            bufs(dec_hidden.shape, BF16),
            bufs(dec_hidden.shape, BF16),
            dma((11,)),
            *[dma((NDP,)) for _ in range(6)],
            *[dma((NGROUP,)) for _ in range(6)],
            dma((4, NGROUP)),
            dma((4, NGROUP)),
            dma((NHEAD,)),
            dma((NHEAD,)),
            dma((2, requests)),
        ],
        compiler_params=pltpu.CompilerParams(
            collective_id=0, has_side_effects=True, vmem_limit_bytes=56 * 2**20
        ),
        cost_estimate=pl.CostEstimate(
            flops=2 * NDP * BLOCK * depth * 2 * COLS, bytes_accessed=24 * 2**20, transcendentals=0
        ),
        name="whole",
    )(block_route, enc_len, dec_query, dec_hidden, memory.reshape(slots, BLOCK, depth), w_key, w_value, w_out)
    return pl.pallas_call(
        hand_on_kernel,
        out_shape=tuple(jax.ShapeDtypeStruct(a.shape, a.dtype) for a in results),
        in_specs=[anywhere] * 3,
        out_specs=(anywhere,) * 3,
        scratch_shapes=[
            bufs((2, requests, span, COLS), BF16),
            bufs(dec_hidden.shape, BF16),
            dma((2, requests)),
            dma((2, requests)),
            dma((2,)),
        ],
        compiler_params=pltpu.CompilerParams(vmem_limit_bytes=56 * 2**20),
        name="hand_on",
    )(*results)


def solution(mesh):
    in_specs = (
        P("dp", None),
        P(None, "dp"),
        P("dp"),
        P(None, "head"),
        P(None, "head"),
        P("dp", "head"),
        P("dp", "head"),
        P("head", None),
    )
    out_specs = (P("dp", "head"), P("dp", None, "head"), P("dp", None, "head"))
    return jax.shard_map(shards, mesh=mesh, in_specs=in_specs, out_specs=out_specs, check_vma=False)
```

```python
import functools

import jax
import jax.numpy as jnp
from jax import lax
from jax.experimental import pallas as pl
from jax.experimental.pallas import tpu as pltpu
from jax.sharding import PartitionSpec as P

HEAD_DIM = 64
BLOCK = 128
MAXB = 4
ZN, YN, XN, CN = 8, 4, 4, 2
NDP, NHEAD = ZN * YN, XN * CN
COLS = 256
DIRECT = 11
GROUP = 1
LAG = 3

SEND = 16
EARLY = 4
NMEM = NDP - DIRECT
NGROUP = NMEM // GROUP
MESH = pl.DeviceIdType.MESH
BF16 = jnp.bfloat16
F32 = jnp.float32


def slot_offset(k):
    outer = (k + NDP - YN) // NDP
    last = k // (NDP - YN)
    middle = outer - last
    m = (k + NDP - YN) % NDP
    dz = middle * (m // 8 + 1) * (1 - 2 * (m % 2)) + last * (ZN // 2) + ZN
    j = (1 - outer) * k + middle * ((m % 8) // 2) + last * (k - NDP + YN)
    turn = 1 - 2 * middle * (m % 2)
    dy = turn * ((j % 2) * ((j + 1) // 2) - (1 - j % 2) * (j // 2)) + YN
    return dz, dy


def each(first, last, act):
    def step(k, _):
        act(k)
        return 0

    lax.fori_loop(first, last, step, 0)


def whole_kernel(
    route_in, lengths_in, query_in, hidden_in, mem, wk, wv, wo, new_hidden, keys, values,
    own, full, wts, wout, packed, kv_out, tag_out, tags, place, pool, kv, key_grid, value_grid,
    score, att, ctx, partial, parts, home_of, cells, route, lengths, query, hidden, summed_hidden,
    in_sem, a_send, a_recv, d_send, d_recv, t_send, t_recv,
    xp_send, xp_recv, xm_send, xm_recv, f_send, f_recv, c_send, c_recv, s_send, s_recv, out_sem,
):
    dp, head = lax.axis_index("dp"), lax.axis_index("head")
    z, y = lax.div(dp, YN), lax.rem(dp, YN)
    x, core = lax.div(head, CN), lax.rem(head, CN)
    right = lax.rem(x + 1, XN) * CN + core
    left = lax.rem(x + XN - 1, XN) * CN + core
    across = lax.rem(x + 2, XN) * CN + core
    twin = x * CN + 1 - core
    slots = mem.shape[0]
    requests = keys.shape[0]

    def peer(k):
        dz, dy = slot_offset(k)
        return lax.rem(z + dz, ZN) * YN + lax.rem(y + dy, YN)

    columns = pl.ds(pl.multiple_of(head * COLS, COLS), COLS)
    get_route = pltpu.make_async_copy(route_in, route, in_sem.at[6])
    get_route.start()
    loads = [
        pltpu.make_async_copy(mem.at[:, :, columns], own, in_sem.at[0]),
        pltpu.make_async_copy(mem, full, in_sem.at[1]),
        pltpu.make_async_copy(wk, wts.at[:, 0:COLS], in_sem.at[2]),
        pltpu.make_async_copy(wv, wts.at[:, COLS : 2 * COLS], in_sem.at[3]),
        pltpu.make_async_copy(wo, wout, in_sem.at[4]),
        pltpu.make_async_copy(lengths_in, lengths, in_sem.at[7]),
        pltpu.make_async_copy(query_in, query, in_sem.at[8]),
        pltpu.make_async_copy(hidden_in, hidden, in_sem.at[9]),
    ]
    for load in loads:
        load.start()

    barrier = pltpu.get_barrier_semaphore()

    for k in range(NDP - 1, 0, -1):
        pl.semaphore_signal(barrier, inc=1, device_id=(peer(k), head), device_id_type=MESH)
    for step in range(1, NHEAD):
        pl.semaphore_signal(barrier, inc=1, device_id=(dp, lax.rem(head + step, NHEAD)), device_id_type=MESH)

    get_route.wait()
    to_home = [route[0, j] for j in range(slots)]

    for k in range(NDP):
        home = peer(k)
        index = jnp.int32(0)
        for j in range(slots):
            index = jnp.where(to_home[j] == home, j, index)
        home_of[k] = index

    loads[0].wait()

    for k in range(DIRECT, NDP):
        packed[k - DIRECT] = own[home_of[k]]
    pl.semaphore_wait(barrier, NDP - 1 + NHEAD - 1)

    def rows_of(g):
        return pl.ds(pl.multiple_of(g * (GROUP * BLOCK), GROUP * BLOCK), GROUP * BLOCK)

    def a_copy(k):
        rows = pl.ds(pl.multiple_of((k - DIRECT) * BLOCK, BLOCK), BLOCK)
        return pltpu.make_async_remote_copy(
            src_ref=packed.at[k - DIRECT], dst_ref=pool.at[head, rows, :],
            send_sem=a_send.at[k], recv_sem=a_recv.at[k],
            device_id=(peer(k), head), device_id_type=MESH)

    def t_copy(k):
        return pltpu.make_async_remote_copy(
            src_ref=tag_out.at[k], dst_ref=tags.at[k],
            send_sem=t_send.at[k], recv_sem=t_recv.at[k],
            device_id=(peer(k), head), device_id_type=MESH)

    def d_copy(k):
        return pltpu.make_async_remote_copy(
            src_ref=kv_out.at[k], dst_ref=kv.at[k],
            send_sem=d_send.at[k], recv_sem=d_recv.at[k],
            device_id=(peer(k), head), device_id_type=MESH)

    for k in range(DIRECT, NDP):
        a_copy(k).start()

    rows_k = lax.broadcasted_iota(jnp.int32, (NDP, 1, 128), 0)
    offset_z, offset_y = slot_offset(rows_k)
    homes = ((z + offset_z) % ZN) * YN + (y + offset_y) % YN
    cell = jnp.full((NDP, 1, 128), -1, jnp.int32)
    for j in range(slots):
        cell = jnp.where(homes == to_home[j], route[1, j], cell)
    tag_out[...] = cell
    tags[0] = cell[0]
    for k in range(1, NDP):
        t_copy(k).start()

    def project(rows):
        return jnp.dot(rows, wts[...], preferred_element_type=F32).astype(BF16)

    def direct_group(g):
        base = g * GROUP
        rows = jnp.concatenate([full[home_of[base + i]] for i in range(GROUP)], axis=0)
        kv_out[pl.ds(base, GROUP)] = project(rows).reshape(GROUP, BLOCK, 2 * COLS)

    def head_copy(piece, group, target, send, recv):
        where = pool.at[piece, rows_of(group), :]
        return pltpu.make_async_remote_copy(
            src_ref=where, dst_ref=where, send_sem=send, recv_sem=recv,
            device_id=(dp, target), device_id_type=MESH)

    def plus_copy(g):
        return head_copy(head, g, right, xp_send.at[g], xp_recv.at[g])

    def minus_copy(g):
        return head_copy(head, g, left, xm_send.at[g], xm_recv.at[g])

    def forward_right(g):
        return head_copy(left, g, right, f_send.at[g], f_recv.at[g])

    def forward_left(g):
        return head_copy(right, g, left, f_send.at[g], f_recv.at[g])

    def core_copy(piece, n, g):
        return head_copy(piece, g, twin, c_send.at[n, g], c_recv.at[n, g])

    def stage_own(g):
        each(DIRECT + g * GROUP, DIRECT + (g + 1) * GROUP, lambda k: a_copy(k).wait_recv())
        plus_copy(g).start()
        minus_copy(g).start()
        core_copy(head, 0, g).start()

    def stage_forward(g):
        plus_copy(g).wait_recv()
        minus_copy(g).wait_recv()
        pl.when(g % 2 == 0)(lambda: forward_right(g).start())
        pl.when(g % 2 == 1)(lambda: forward_left(g).start())
        core_copy(left, 1, g).start()
        core_copy(right, 2, g).start()

    def stage_core(g):
        forward_right(g).wait_recv()
        core_copy(across, 3, g).start()

    def stage_project(g):
        for n in range(4):
            core_copy(head, n, g).wait_recv()
        rows = jnp.concatenate([pool[p, rows_of(g), :] for p in range(NHEAD)], axis=1)
        kv[pl.ds(DIRECT + g * GROUP, GROUP)] = project(rows).reshape(GROUP, BLOCK, 2 * COLS)

    def round_of(t):
        def weights():
            for load in loads[1:]:
                load.wait()

        pl.when(t == EARLY)(weights)
        for late, stage in enumerate((stage_own, stage_forward, stage_core, stage_project)):
            g = t - late * LAG
            pl.when((g >= 0) & (g < NGROUP))(functools.partial(stage, g))
        def send_direct():
            for k in range(1, DIRECT):
                d_copy(k).start()

        pl.when(t == SEND)(send_direct)
        n = t - EARLY
        pl.when((n >= 0) & (n < DIRECT // GROUP))(lambda: direct_group(n))

    each(0, NGROUP + 2 * LAG, round_of)

    each(1, NDP, lambda k: t_copy(k).wait_recv())
    lane = lax.broadcasted_iota(jnp.int32, (NDP, 1, 128), 2)
    slot = lax.broadcasted_iota(jnp.int32, (NDP, 1, 128), 0)
    place[...] = jnp.max(jnp.where(tags[...] == lane, slot, 0), axis=0)
    to_scalars = pltpu.make_async_copy(place, cells, in_sem.at[5])
    to_scalars.start()

    each(NGROUP + 2 * LAG, NGROUP + 3 * LAG, round_of)
    kv[0] = kv_out[0]
    each(1, DIRECT, lambda k: d_copy(k).wait_recv())
    to_scalars.wait()

    span = MAXB * BLOCK
    outs = []
    for r in range(requests):
        for b in range(MAXB):
            block = kv[cells[0, r * MAXB + b]]
            block = jnp.where(lengths[r] > b * BLOCK, block, jnp.zeros_like(block))
            key_grid[r, b * BLOCK : (b + 1) * BLOCK, :] = block[:, 0:COLS]
            value_grid[r, b * BLOCK : (b + 1) * BLOCK, :] = block[:, COLS : 2 * COLS]
        outs.append(pltpu.make_async_copy(key_grid.at[r], keys.at[r], out_sem.at[0, r]))
        outs.append(pltpu.make_async_copy(value_grid.at[r], values.at[r], out_sem.at[1, r]))
        for copy in outs[-2:]:
            copy.start()

    own_head = lax.broadcasted_iota(jnp.int32, (8, COLS), 1) // HEAD_DIM == lax.broadcasted_iota(
        jnp.int32, (8, COLS), 0
    )
    position = lax.broadcasted_iota(jnp.int32, (8, span), 1)
    for r in range(requests):
        spread = jnp.where(own_head, jnp.broadcast_to(query[r : r + 1, :].astype(F32), (8, COLS)), 0.0)
        dots = lax.dot_general(
            spread.astype(BF16), key_grid[r], (((1,), (1,)), ((), ())), preferred_element_type=F32
        )
        score[r * 8 : (r + 1) * 8, :] = jnp.where(position < lengths[r], dots, -1e30)
    scores = score[...]
    expo = jnp.exp(scores - jnp.max(scores, axis=1, keepdims=True))
    att[...] = (expo / jnp.sum(expo, axis=1, keepdims=True)).astype(BF16)
    ctx[...] = jnp.zeros_like(ctx)
    for r in range(requests):
        mixed = jnp.dot(att[r * 8 : (r + 1) * 8, :], value_grid[r], preferred_element_type=F32)
        ctx[r : r + 1, :] = jnp.sum(jnp.where(own_head, mixed, 0.0), axis=0, keepdims=True)
    summed = jnp.dot(ctx[...].astype(BF16), wout[...], preferred_element_type=F32)
    for p in range(NHEAD):
        partial[p] = summed[:, p * COLS : (p + 1) * COLS]

    def s_copy(step):
        other = lax.rem(head + step, NHEAD)
        return pltpu.make_async_remote_copy(
            src_ref=partial.at[other], dst_ref=parts.at[step],
            send_sem=s_send.at[step], recv_sem=s_recv.at[step],
            device_id=(dp, other), device_id_type=MESH)

    for step in range(1, NHEAD):
        s_copy(step).start()

    each(DIRECT, NDP, lambda k: a_copy(k).wait_send())
    each(1, DIRECT, lambda k: d_copy(k).wait_send())
    each(1, NDP, lambda k: t_copy(k).wait_send())

    def settle_group(g):
        plus_copy(g).wait_send()
        minus_copy(g).wait_send()
        forward_right(g).wait_send()
        for n in range(4):
            core_copy(head, n, g).wait_send()

    each(0, NGROUP, settle_group)

    total = partial[head]
    for step in range(1, NHEAD):
        s_copy(step).wait_recv()
        total = total + parts[step]
    summed_hidden[...] = (hidden[...].astype(F32) + total[0:requests, :]).astype(BF16)
    outs.append(pltpu.make_async_copy(summed_hidden, new_hidden, in_sem.at[10]))
    outs[-1].start()
    for step in range(1, NHEAD):
        s_copy(step).wait_send()
    for copy in outs:
        copy.wait()


def hand_on_kernel(hidden_in, keys_in, values_in, hidden, keys, values, staged, small, in_sem, out_sem, small_sem):
    requests = keys.shape[0]
    steps = [(i, r) for r in range(requests) for i in range(2)]
    takes, gives = [], []
    for i, r in steps:
        source, target = (keys_in, keys) if i == 0 else (values_in, values)
        takes.append(pltpu.make_async_copy(source.at[r], staged.at[i, r], in_sem.at[i, r]))
        gives.append(pltpu.make_async_copy(staged.at[i, r], target.at[r], out_sem.at[i, r]))
    get_small = pltpu.make_async_copy(hidden_in, small, small_sem.at[0])
    put_small = pltpu.make_async_copy(small, hidden, small_sem.at[1])
    get_small.start()
    for take in takes:
        take.start()
    get_small.wait()
    put_small.start()
    for take, give in zip(takes, gives):
        take.wait()
        give.start()
    for give in gives:
        give.wait()
    put_small.wait()


def shards(memory, block_route, enc_len, w_key, w_value, dec_query, dec_hidden, w_out):
    slots, depth, requests = block_route.shape[1], memory.shape[1], enc_len.shape[0]
    span = MAXB * BLOCK
    dma, bufs = pltpu.SemaphoreType.DMA, pltpu.VMEM
    anywhere = pl.BlockSpec(memory_space=pl.ANY)
    grid = jax.ShapeDtypeStruct((requests, span, COLS), BF16)
    results = pl.pallas_call(
        whole_kernel,
        out_shape=(jax.ShapeDtypeStruct(dec_hidden.shape, BF16), grid, grid),
        in_specs=[anywhere] * 8,
        out_specs=(anywhere, anywhere, anywhere),
        scratch_shapes=[
            bufs((slots, BLOCK, COLS), BF16),
            bufs((slots, BLOCK, depth), BF16),
            bufs((depth, 2 * COLS), BF16),
            bufs((COLS, depth), BF16),
            bufs((NMEM, BLOCK, COLS), BF16),
            bufs((DIRECT, BLOCK, 2 * COLS), BF16),
            bufs((NDP, 1, 128), jnp.int32),
            bufs((NDP, 1, 128), jnp.int32),
            bufs((1, 128), jnp.int32),
            bufs((NHEAD, NMEM * BLOCK, COLS), BF16),
            bufs((NDP, BLOCK, 2 * COLS), BF16),
            bufs((requests, span, COLS), BF16),
            bufs((requests, span, COLS), BF16),
            bufs((requests * 8, span), F32),
            bufs((requests * 8, span), BF16),
            bufs((8, COLS), F32),
            bufs((NHEAD, 8, COLS), F32),
            bufs((NHEAD, 8, COLS), F32),
            pltpu.SMEM((NDP,), jnp.int32),
            pltpu.SMEM((1, 128), jnp.int32),
            pltpu.SMEM(block_route.shape, jnp.int32),
            pltpu.SMEM(enc_len.shape, jnp.int32),
            bufs(dec_query.shape, BF16),
            bufs(dec_hidden.shape, BF16),
            bufs(dec_hidden.shape, BF16),
            dma((11,)),
            *[dma((NDP,)) for _ in range(6)],
            *[dma((NGROUP,)) for _ in range(6)],
            dma((4, NGROUP)),
            dma((4, NGROUP)),
            dma((NHEAD,)),
            dma((NHEAD,)),
            dma((2, requests)),
        ],
        compiler_params=pltpu.CompilerParams(
            collective_id=0, has_side_effects=True, vmem_limit_bytes=56 * 2**20
        ),
        cost_estimate=pl.CostEstimate(
            flops=2 * NDP * BLOCK * depth * 2 * COLS, bytes_accessed=24 * 2**20, transcendentals=0
        ),
        name="whole",
    )(block_route, enc_len, dec_query, dec_hidden, memory.reshape(slots, BLOCK, depth), w_key, w_value, w_out)
    return pl.pallas_call(
        hand_on_kernel,
        out_shape=tuple(jax.ShapeDtypeStruct(a.shape, a.dtype) for a in results),
        in_specs=[anywhere] * 3,
        out_specs=(anywhere,) * 3,
        scratch_shapes=[
            bufs((2, requests, span, COLS), BF16),
            bufs(dec_hidden.shape, BF16),
            dma((2, requests)),
            dma((2, requests)),
            dma((2,)),
        ],
        compiler_params=pltpu.CompilerParams(vmem_limit_bytes=56 * 2**20),
        name="hand_on",
    )(*results)


def solution(mesh):
    in_specs = (
        P("dp", None),
        P(None, "dp"),
        P("dp"),
        P(None, "head"),
        P(None, "head"),
        P("dp", "head"),
        P("dp", "head"),
        P("head", None),
    )
    out_specs = (P("dp", "head"), P("dp", None, "head"), P("dp", None, "head"))
    return jax.shard_map(shards, mesh=mesh, in_specs=in_specs, out_specs=out_specs, check_vma=False)
```

```python
import functools

import jax
import jax.numpy as jnp
from jax import lax
from jax.experimental import pallas as pl
from jax.experimental.pallas import tpu as pltpu
from jax.sharding import PartitionSpec as P

HEAD_DIM = 64
BLOCK = 128
MAXB = 4
ZN, YN, XN, CN = 8, 4, 4, 2
NDP, NHEAD = ZN * YN, XN * CN
COLS = 256
DIRECT = 11
GROUP = 1
LAG = 3

SEND = 16
EARLY = 4
NMEM = NDP - DIRECT
NGROUP = NMEM // GROUP
MESH = pl.DeviceIdType.MESH
BF16 = jnp.bfloat16
F32 = jnp.float32


def slot_offset(k):
    outer = (k + NDP - YN) // NDP
    last = k // (NDP - YN)
    middle = outer - last
    m = (k + NDP - YN) % NDP
    dz = middle * (m // 8 + 1) * (1 - 2 * (m % 2)) + last * (ZN // 2) + ZN
    j = (1 - outer) * k + middle * ((m % 8) // 2) + last * (k - NDP + YN)
    turn = 1 - 2 * middle * (m % 2)
    dy = turn * ((j % 2) * ((j + 1) // 2) - (1 - j % 2) * (j // 2)) + YN
    return dz, dy


def each(first, last, act):
    def step(k, _):
        act(k)
        return 0

    lax.fori_loop(first, last, step, 0)


def whole_kernel(
    route_in, lengths_in, query_in, hidden_in, mem, wk, wv, wo, new_hidden, keys, values,
    own, full, wts, wout, packed, kv_out, tag_out, tags, place, pool, kv, key_grid, value_grid,
    score, att, ctx, partial, parts, home_of, cells, route, lengths, query, hidden, summed_hidden,
    in_sem, a_send, a_recv, d_send, d_recv, t_send, t_recv,
    xp_send, xp_recv, xm_send, xm_recv, f_send, f_recv, c_send, c_recv, s_send, s_recv, out_sem,
):
    dp, head = lax.axis_index("dp"), lax.axis_index("head")
    z, y = lax.div(dp, YN), lax.rem(dp, YN)
    x, core = lax.div(head, CN), lax.rem(head, CN)
    right = lax.rem(x + 1, XN) * CN + core
    left = lax.rem(x + XN - 1, XN) * CN + core
    across = lax.rem(x + 2, XN) * CN + core
    twin = x * CN + 1 - core
    slots = mem.shape[0]
    requests = keys.shape[0]

    def peer(k):
        dz, dy = slot_offset(k)
        return lax.rem(z + dz, ZN) * YN + lax.rem(y + dy, YN)

    columns = pl.ds(pl.multiple_of(head * COLS, COLS), COLS)
    get_route = pltpu.make_async_copy(route_in, route, in_sem.at[6])
    get_route.start()
    loads = [
        pltpu.make_async_copy(mem.at[:, :, columns], own, in_sem.at[0]),
        pltpu.make_async_copy(mem, full, in_sem.at[1]),
        pltpu.make_async_copy(wk, wts.at[:, 0:COLS], in_sem.at[2]),
        pltpu.make_async_copy(wv, wts.at[:, COLS : 2 * COLS], in_sem.at[3]),
        pltpu.make_async_copy(wo, wout, in_sem.at[4]),
        pltpu.make_async_copy(lengths_in, lengths, in_sem.at[7]),
        pltpu.make_async_copy(query_in, query, in_sem.at[8]),
        pltpu.make_async_copy(hidden_in, hidden, in_sem.at[9]),
    ]
    for load in loads:
        load.start()

    barrier = pltpu.get_barrier_semaphore()

    for k in range(NDP - 1, 0, -1):
        pl.semaphore_signal(barrier, inc=1, device_id=(peer(k), head), device_id_type=MESH)
    for step in range(1, NHEAD):
        pl.semaphore_signal(barrier, inc=1, device_id=(dp, lax.rem(head + step, NHEAD)), device_id_type=MESH)

    get_route.wait()
    to_home = [route[0, j] for j in range(slots)]

    for k in range(NDP):
        home = peer(k)
        index = jnp.int32(0)
        for j in range(slots):
            index = jnp.where(to_home[j] == home, j, index)
        home_of[k] = index

    loads[0].wait()

    for k in range(DIRECT, NDP):
        packed[k - DIRECT] = own[home_of[k]]
    pl.semaphore_wait(barrier, NDP - 1 + NHEAD - 1)

    def rows_of(g):
        return pl.ds(pl.multiple_of(g * (GROUP * BLOCK), GROUP * BLOCK), GROUP * BLOCK)

    def a_copy(k):
        rows = pl.ds(pl.multiple_of((k - DIRECT) * BLOCK, BLOCK), BLOCK)
        return pltpu.make_async_remote_copy(
            src_ref=packed.at[k - DIRECT], dst_ref=pool.at[head, rows, :],
            send_sem=a_send.at[k], recv_sem=a_recv.at[k],
            device_id=(peer(k), head), device_id_type=MESH)

    def t_copy(k):
        return pltpu.make_async_remote_copy(
            src_ref=tag_out.at[k], dst_ref=tags.at[k],
            send_sem=t_send.at[k], recv_sem=t_recv.at[k],
            device_id=(peer(k), head), device_id_type=MESH)

    def d_copy(k):
        return pltpu.make_async_remote_copy(
            src_ref=kv_out.at[k], dst_ref=kv.at[k],
            send_sem=d_send.at[k], recv_sem=d_recv.at[k],
            device_id=(peer(k), head), device_id_type=MESH)

    for k in range(DIRECT, NDP):
        a_copy(k).start()

    rows_k = lax.broadcasted_iota(jnp.int32, (NDP, 1, 128), 0)
    offset_z, offset_y = slot_offset(rows_k)
    homes = ((z + offset_z) % ZN) * YN + (y + offset_y) % YN
    cell = jnp.full((NDP, 1, 128), -1, jnp.int32)
    for j in range(slots):
        cell = jnp.where(homes == to_home[j], route[1, j], cell)
    tag_out[...] = cell
    tags[0] = cell[0]
    for k in range(1, NDP):
        t_copy(k).start()

    def project(rows):
        return jnp.dot(rows, wts[...], preferred_element_type=F32).astype(BF16)

    def direct_group(g):
        base = g * GROUP
        rows = jnp.concatenate([full[home_of[base + i]] for i in range(GROUP)], axis=0)
        kv_out[pl.ds(base, GROUP)] = project(rows).reshape(GROUP, BLOCK, 2 * COLS)

    def head_copy(piece, group, target, send, recv):
        where = pool.at[piece, rows_of(group), :]
        return pltpu.make_async_remote_copy(
            src_ref=where, dst_ref=where, send_sem=send, recv_sem=recv,
            device_id=(dp, target), device_id_type=MESH)

    def plus_copy(g):
        return head_copy(head, g, right, xp_send.at[g], xp_recv.at[g])

    def minus_copy(g):
        return head_copy(head, g, left, xm_send.at[g], xm_recv.at[g])

    def forward_right(g):
        return head_copy(left, g, right, f_send.at[g], f_recv.at[g])

    def forward_left(g):
        return head_copy(right, g, left, f_send.at[g], f_recv.at[g])

    def core_copy(piece, n, g):
        return head_copy(piece, g, twin, c_send.at[n, g], c_recv.at[n, g])

    def stage_own(g):
        each(DIRECT + g * GROUP, DIRECT + (g + 1) * GROUP, lambda k: a_copy(k).wait_recv())
        plus_copy(g).start()
        minus_copy(g).start()
        core_copy(head, 0, g).start()

    def stage_forward(g):
        plus_copy(g).wait_recv()
        minus_copy(g).wait_recv()
        pl.when(g % 2 == 0)(lambda: forward_right(g).start())
        pl.when(g % 2 == 1)(lambda: forward_left(g).start())
        core_copy(left, 1, g).start()
        core_copy(right, 2, g).start()

    def stage_core(g):
        forward_right(g).wait_recv()
        core_copy(across, 3, g).start()

    def stage_project(g):
        for n in range(4):
            core_copy(head, n, g).wait_recv()
        rows = jnp.concatenate([pool[p, rows_of(g), :] for p in range(NHEAD)], axis=1)
        kv[pl.ds(DIRECT + g * GROUP, GROUP)] = project(rows).reshape(GROUP, BLOCK, 2 * COLS)

    def round_of(t):
        def weights():
            for load in loads[1:]:
                load.wait()

        pl.when(t == EARLY)(weights)
        for late, stage in ((1, stage_forward), (2, stage_core), (0, stage_own), (3, stage_project)):
            g = t - late * LAG
            pl.when((g >= 0) & (g < NGROUP))(functools.partial(stage, g))
        def send_direct():
            for k in range(1, DIRECT):
                d_copy(k).start()

        pl.when(t == SEND)(send_direct)
        n = t - EARLY
        pl.when((n >= 0) & (n < DIRECT // GROUP))(lambda: direct_group(n))

    each(0, NGROUP + 2 * LAG, round_of)

    each(1, NDP, lambda k: t_copy(k).wait_recv())
    lane = lax.broadcasted_iota(jnp.int32, (NDP, 1, 128), 2)
    slot = lax.broadcasted_iota(jnp.int32, (NDP, 1, 128), 0)
    place[...] = jnp.max(jnp.where(tags[...] == lane, slot, 0), axis=0)
    to_scalars = pltpu.make_async_copy(place, cells, in_sem.at[5])
    to_scalars.start()

    each(NGROUP + 2 * LAG, NGROUP + 3 * LAG, round_of)
    kv[0] = kv_out[0]
    each(1, DIRECT, lambda k: d_copy(k).wait_recv())
    to_scalars.wait()

    span = MAXB * BLOCK
    outs = []
    for r in range(requests):
        for b in range(MAXB):
            block = kv[cells[0, r * MAXB + b]]
            block = jnp.where(lengths[r] > b * BLOCK, block, jnp.zeros_like(block))
            key_grid[r, b * BLOCK : (b + 1) * BLOCK, :] = block[:, 0:COLS]
            value_grid[r, b * BLOCK : (b + 1) * BLOCK, :] = block[:, COLS : 2 * COLS]
        outs.append(pltpu.make_async_copy(key_grid.at[r], keys.at[r], out_sem.at[0, r]))
        outs.append(pltpu.make_async_copy(value_grid.at[r], values.at[r], out_sem.at[1, r]))
        for copy in outs[-2:]:
            copy.start()

    own_head = lax.broadcasted_iota(jnp.int32, (8, COLS), 1) // HEAD_DIM == lax.broadcasted_iota(
        jnp.int32, (8, COLS), 0
    )
    position = lax.broadcasted_iota(jnp.int32, (8, span), 1)
    for r in range(requests):
        spread = jnp.where(own_head, jnp.broadcast_to(query[r : r + 1, :].astype(F32), (8, COLS)), 0.0)
        dots = lax.dot_general(
            spread.astype(BF16), key_grid[r], (((1,), (1,)), ((), ())), preferred_element_type=F32
        )
        score[r * 8 : (r + 1) * 8, :] = jnp.where(position < lengths[r], dots, -1e30)
    scores = score[...]
    expo = jnp.exp(scores - jnp.max(scores, axis=1, keepdims=True))
    att[...] = (expo / jnp.sum(expo, axis=1, keepdims=True)).astype(BF16)
    ctx[...] = jnp.zeros_like(ctx)
    for r in range(requests):
        mixed = jnp.dot(att[r * 8 : (r + 1) * 8, :], value_grid[r], preferred_element_type=F32)
        ctx[r : r + 1, :] = jnp.sum(jnp.where(own_head, mixed, 0.0), axis=0, keepdims=True)
    summed = jnp.dot(ctx[...].astype(BF16), wout[...], preferred_element_type=F32)
    for p in range(NHEAD):
        partial[p] = summed[:, p * COLS : (p + 1) * COLS]

    def s_copy(step):
        other = lax.rem(head + step, NHEAD)
        return pltpu.make_async_remote_copy(
            src_ref=partial.at[other], dst_ref=parts.at[step],
            send_sem=s_send.at[step], recv_sem=s_recv.at[step],
            device_id=(dp, other), device_id_type=MESH)

    for step in range(1, NHEAD):
        s_copy(step).start()

    each(DIRECT, NDP, lambda k: a_copy(k).wait_send())
    each(1, DIRECT, lambda k: d_copy(k).wait_send())
    each(1, NDP, lambda k: t_copy(k).wait_send())

    def settle_group(g):
        plus_copy(g).wait_send()
        minus_copy(g).wait_send()
        forward_right(g).wait_send()
        for n in range(4):
            core_copy(head, n, g).wait_send()

    each(0, NGROUP, settle_group)

    total = partial[head]
    for step in range(1, NHEAD):
        s_copy(step).wait_recv()
        total = total + parts[step]
    summed_hidden[...] = (hidden[...].astype(F32) + total[0:requests, :]).astype(BF16)
    outs.append(pltpu.make_async_copy(summed_hidden, new_hidden, in_sem.at[10]))
    outs[-1].start()
    for step in range(1, NHEAD):
        s_copy(step).wait_send()
    for copy in outs:
        copy.wait()


def hand_on_kernel(hidden_in, keys_in, values_in, hidden, keys, values, staged, small, in_sem, out_sem, small_sem):
    requests = keys.shape[0]
    steps = [(i, r) for r in range(requests) for i in range(2)]
    takes, gives = [], []
    for i, r in steps:
        source, target = (keys_in, keys) if i == 0 else (values_in, values)
        takes.append(pltpu.make_async_copy(source.at[r], staged.at[i, r], in_sem.at[i, r]))
        gives.append(pltpu.make_async_copy(staged.at[i, r], target.at[r], out_sem.at[i, r]))
    get_small = pltpu.make_async_copy(hidden_in, small, small_sem.at[0])
    put_small = pltpu.make_async_copy(small, hidden, small_sem.at[1])
    get_small.start()
    for take in takes:
        take.start()
    get_small.wait()
    put_small.start()
    for take, give in zip(takes, gives):
        take.wait()
        give.start()
    for give in gives:
        give.wait()
    put_small.wait()


def shards(memory, block_route, enc_len, w_key, w_value, dec_query, dec_hidden, w_out):
    slots, depth, requests = block_route.shape[1], memory.shape[1], enc_len.shape[0]
    span = MAXB * BLOCK
    dma, bufs = pltpu.SemaphoreType.DMA, pltpu.VMEM
    anywhere = pl.BlockSpec(memory_space=pl.ANY)
    grid = jax.ShapeDtypeStruct((requests, span, COLS), BF16)
    results = pl.pallas_call(
        whole_kernel,
        out_shape=(jax.ShapeDtypeStruct(dec_hidden.shape, BF16), grid, grid),
        in_specs=[anywhere] * 8,
        out_specs=(anywhere, anywhere, anywhere),
        scratch_shapes=[
            bufs((slots, BLOCK, COLS), BF16),
            bufs((slots, BLOCK, depth), BF16),
            bufs((depth, 2 * COLS), BF16),
            bufs((COLS, depth), BF16),
            bufs((NMEM, BLOCK, COLS), BF16),
            bufs((DIRECT, BLOCK, 2 * COLS), BF16),
            bufs((NDP, 1, 128), jnp.int32),
            bufs((NDP, 1, 128), jnp.int32),
            bufs((1, 128), jnp.int32),
            bufs((NHEAD, NMEM * BLOCK, COLS), BF16),
            bufs((NDP, BLOCK, 2 * COLS), BF16),
            bufs((requests, span, COLS), BF16),
            bufs((requests, span, COLS), BF16),
            bufs((requests * 8, span), F32),
            bufs((requests * 8, span), BF16),
            bufs((8, COLS), F32),
            bufs((NHEAD, 8, COLS), F32),
            bufs((NHEAD, 8, COLS), F32),
            pltpu.SMEM((NDP,), jnp.int32),
            pltpu.SMEM((1, 128), jnp.int32),
            pltpu.SMEM(block_route.shape, jnp.int32),
            pltpu.SMEM(enc_len.shape, jnp.int32),
            bufs(dec_query.shape, BF16),
            bufs(dec_hidden.shape, BF16),
            bufs(dec_hidden.shape, BF16),
            dma((11,)),
            *[dma((NDP,)) for _ in range(6)],
            *[dma((NGROUP,)) for _ in range(6)],
            dma((4, NGROUP)),
            dma((4, NGROUP)),
            dma((NHEAD,)),
            dma((NHEAD,)),
            dma((2, requests)),
        ],
        compiler_params=pltpu.CompilerParams(
            collective_id=0, has_side_effects=True, vmem_limit_bytes=56 * 2**20
        ),
        cost_estimate=pl.CostEstimate(
            flops=2 * NDP * BLOCK * depth * 2 * COLS, bytes_accessed=24 * 2**20, transcendentals=0
        ),
        name="whole",
    )(block_route, enc_len, dec_query, dec_hidden, memory.reshape(slots, BLOCK, depth), w_key, w_value, w_out)
    return pl.pallas_call(
        hand_on_kernel,
        out_shape=tuple(jax.ShapeDtypeStruct(a.shape, a.dtype) for a in results),
        in_specs=[anywhere] * 3,
        out_specs=(anywhere,) * 3,
        scratch_shapes=[
            bufs((2, requests, span, COLS), BF16),
            bufs(dec_hidden.shape, BF16),
            dma((2, requests)),
            dma((2, requests)),
            dma((2,)),
        ],
        compiler_params=pltpu.CompilerParams(vmem_limit_bytes=56 * 2**20),
        name="hand_on",
    )(*results)


def solution(mesh):
    in_specs = (
        P("dp", None),
        P(None, "dp"),
        P("dp"),
        P(None, "head"),
        P(None, "head"),
        P("dp", "head"),
        P("dp", "head"),
        P("head", None),
    )
    out_specs = (P("dp", "head"), P("dp", None, "head"), P("dp", None, "head"))
    return jax.shard_map(shards, mesh=mesh, in_specs=in_specs, out_specs=out_specs, check_vma=False)
```
